32 devices in a mesh: dp: 4 (over y, x), label: 8 (over z, core).
Axes of the slice: x: 2, y: 2, z: 4, core: 2. Of those that a mesh axis runs over, the one named last changes fastest.
Arguments:
- encoded: bfloat16 [8192, 768], P(('dp', 'label')), may hold values from -8 to 8
- coarse_weight: bfloat16 [512, 768], P(('dp', 'label')), may hold values from -1 to 1
- fine_weight: bfloat16 [512, 128, 768], P(('dp', 'label')), may hold values from -0.21875 to 0.21875
- cluster_group: int32 [8192, 8], P(('dp', 'label')), may hold values from 0 to 31, all different within a row; in each aligned block of 256 rows (0 to 255, 256 to 511, ...) at most 96 rows name the same one
- cluster_member: int32 [8192, 8], P(('dp', 'label')), may hold values from 0 to 15
- positive: int32 [8192], P(('dp', 'label')), may hold values from 0 to 127
Outputs:
- row_loss: float32 [8192], P(('dp', 'label'))
- d_encoded: bfloat16 [8192, 768], P(('dp', 'label'))
- d_fine: bfloat16 [512, 128, 768], P(('dp', 'label'))
- cluster_loss: float32 [512], P(('dp', 'label'))
The draws below stay inside these ranges and needn't reach their ends.
Inputs may be any that keep to these rules, and one draw needn't show every extreme that they name: `cluster_group`: each row names 8 different groups. Among the rows of one device (aligned blocks of 256 rows) no group is named by more than 96 rows, a bound that some block reaches.
All inputs are finite; a program needn't handle non-finite values.
Results may differ from the reference program's by a relative error of at most 0.0051.
Values may be sent and summed in bfloat16 or wider, within the bound.
A program may use at most 128 MiB of HBM per device.

```python
import math
import jax
import jax.numpy as jnp
import numpy as np
from jax import lax

D = 768
LBL = 128
TOP = 8
CL_DEV = 16
ROW_DEV = 256
ROWS = 8192
CLUSTERS = 512
CAP = 96
N_DP = 4
N_LABEL = 8


def draw_encoded(key, part):
    drawn = jax.random.normal(jax.random.fold_in(key, 11), (ROWS, D), jnp.float32)
    return jnp.clip(drawn, -8.0, 8.0).astype(jnp.bfloat16)


def draw_coarse_weight(key, part):
    drawn = jax.random.normal(jax.random.fold_in(key, 21), (CLUSTERS, D), jnp.float32) / math.sqrt(D)
    scales = jnp.exp(jax.random.uniform(jax.random.fold_in(key, 22), (CLUSTERS, 1), jnp.float32, math.log(0.3), math.log(3.0)))
    weight = drawn * scales
    return jnp.clip(weight, -1.0, 1.0).astype(jnp.bfloat16)


def touch_ends(drawn, own_key, low, high):
    place = [jax.random.randint(jax.random.fold_in(own_key, axis), (), 0, length) for axis, length in enumerate(drawn.shape)]
    widest = drawn.shape.index(max(drawn.shape))
    next_to = place[:widest] + [(place[widest] + 1) % drawn.shape[widest]] + place[widest + 1:]
    return drawn.at[tuple(place)].set(low).at[tuple(next_to)].set(high)


def block_scale(own_key, extent, cuts, low, high):
    def one(dim, shards_of):
        draws = jax.random.uniform(jax.random.fold_in(jax.random.fold_in(own_key, 6), dim), (shards_of,), jnp.float32, low / len(cuts), high / len(cuts))
        return jnp.repeat(jnp.exp(draws), extent[dim] // shards_of).reshape((-1,) + (1,) * (len(extent) - dim - 1))

    loudness = one(*cuts[0])
    for cut in cuts[1:]:
        loudness = loudness * one(*cut)
    return loudness


def assign_block(own_key, own, number, rows, amount, top, most, skew):
    ranking = jax.random.permutation(own_key, amount)
    crowded, usual = portions_of(amount, rows * top, most, skew, True), portions_of(amount, rows * top, most, skew, False)
    places = jnp.arange(amount)

    def named(tallies, offset_by):
        used = int((tallies > 0).sum())
        fixed = max(1, used // 4)
        shifted = fixed + (places - fixed + offset_by * (used - fixed)) % max(1, amount - fixed)
        return jnp.zeros((amount,), jnp.int32).at[ranking[jnp.where(places < fixed, places, shifted)]].set(jnp.asarray(tallies, jnp.int32))

    tallies = jnp.where(number % 4 == 0, named(crowded, number // 4), named(usual, number - number // 4 - 1))
    mixed = jax.random.permutation(jax.random.fold_in(own, 3), amount)
    source_of, receiver = mixed[0:amount // 2 * 2:2], mixed[1:amount // 2 * 2:2]
    margin = jnp.minimum(tallies[source_of] - 1, most - tallies[receiver]) // 2
    margin = jnp.where((source_of == ranking[0]) | (receiver == ranking[0]) | (tallies[receiver] == 0), 0, jnp.maximum(margin, 0))
    shifted = jax.random.randint(jax.random.fold_in(own, 4), (amount // 2,), 0, 1 << 20) % (margin + 1)
    tallies = tallies.at[source_of].add(-shifted).at[receiver].add(shifted)
    labels = jnp.searchsorted(jnp.cumsum(tallies), jnp.arange(rows * top), side="right").astype(jnp.int32)
    listing = labels.reshape(top, rows).T
    listing = listing[jax.random.permutation(jax.random.fold_in(own, 1), rows)]
    offset_by = jax.random.randint(jax.random.fold_in(own, 2), (rows, 1), 0, top)
    return jnp.take_along_axis(listing, (jnp.arange(top)[None, :] + offset_by) % top, axis=1)


def portions_of(count, total, reach, lean, full):
    weights = [(1 << 20) // math.isqrt(grade ** lean) + 1 for grade in range(1, count + 1)]
    largest = reach if full else min(reach, max(-(-total // count), total * weights[0] // sum(weights)))
    least = 1 if total - largest >= count - 1 else 0
    holding, spare = [largest] + [least] * (count - 1), total - largest - least * (count - 1)
    while spare > 0:
        free = [i for i in range(1, count) if holding[i] < largest] or [i for i in range(1, count) if holding[i] < reach]
        mass, remaining = sum([weights[i] for i in free]), spare
        for i in free:
            more = min(reach - holding[i], max(1, remaining * weights[i] // mass), spare)
            holding[i] = holding[i] + more
            spare = spare - more
    return np.array(holding)


def normal_values(rng, dims, spread, reach, split=(), kind=jnp.bfloat16):
    entries = spread * jax.random.normal(rng, dims, jnp.float32)
    if split:
        entries = entries * block_scale(rng, dims, split, -0.22, 0.18)
    return jnp.clip(entries, -reach, reach).astype(kind)


def setup_inputs(seed: int = 0) -> dict:
    key_list = jax.random.split(jax.random.key(seed), 7)
    encoded = draw_encoded(jax.random.fold_in(key_list[6], 71), 0)
    coarse_weight = draw_coarse_weight(jax.random.fold_in(key_list[6], 71), 0)
    fine_weight = normal_values(key_list[2], (CLUSTERS, LBL, D), D ** -0.5, 0.21875, ((0, 32),))
    cluster_group_keys = jax.random.split(jax.random.fold_in(key_list[3], 1), ROWS // ROW_DEV)
    cluster_group_turns = jax.random.permutation(jax.random.fold_in(key_list[3], 3), ROWS // ROW_DEV)
    cluster_group = jax.vmap(lambda own, number: assign_block(jax.random.fold_in(key_list[3], 2), own, number, ROW_DEV, N_DP * N_LABEL, TOP, CAP, 2))(cluster_group_keys, cluster_group_turns).reshape((ROWS, TOP))
    cluster_member = touch_ends(jax.random.randint(key_list[4], (ROWS, TOP), 0, CL_DEV), jax.random.fold_in(key_list[4], 1), 0, CL_DEV - 1).astype(jnp.int32)
    positive = touch_ends(jax.random.randint(key_list[5], (ROWS,), 0, LBL), jax.random.fold_in(key_list[5], 1), 0, LBL - 1).astype(jnp.int32)
    return dict(encoded=encoded, coarse_weight=coarse_weight, fine_weight=fine_weight, cluster_group=cluster_group, cluster_member=cluster_member, positive=positive)


def softplus_loss(logits, truth):
    return jnp.maximum(logits, 0.0) + jnp.log1p(jnp.exp(-jnp.abs(logits))) - truth * logits


def reference(encoded, coarse_weight, fine_weight, cluster_group, cluster_member, positive):
    cluster = cluster_group * CL_DEV + cluster_member
    target = cluster[:, 0]
    row_total = encoded.shape[0]
    block_rows = 256
    clusters_all = coarse_weight.shape[0]
    column_ids = jnp.arange(clusters_all, dtype=jnp.int32)

    def coarse_block(pieces):
        rows_block, target_block = pieces
        scores = jnp.dot(rows_block, coarse_weight.T, preferred_element_type=jnp.float32)
        top_score = jnp.max(scores, axis=1, keepdims=True)
        logsum = top_score[:, 0] + jnp.log(jnp.sum(jnp.exp(scores - top_score), axis=1))
        is_target = column_ids[None, :] == target_block[:, None]
        target_score = jnp.sum(jnp.where(is_target, scores, 0.0), axis=1)
        grad_block = (jnp.exp(scores - logsum[:, None]) - is_target.astype(jnp.float32)).astype(jnp.bfloat16)
        back_block = jnp.dot(grad_block, coarse_weight, preferred_element_type=jnp.float32)
        return logsum - target_score, back_block

    row_loss, coarse_back = lax.map(coarse_block, (encoded.reshape(-1, block_rows, D), target.reshape(-1, block_rows)))
    row_loss = row_loss.reshape(row_total)
    coarse_back = coarse_back.reshape(row_total, D)

    slot_total = row_total * TOP
    keys = cluster.reshape(-1).astype(jnp.int32)
    sorted_index = jnp.argsort(keys, stable=True).astype(jnp.int32)
    counts = jax.ops.segment_sum(jnp.ones(slot_total, jnp.int32), keys, num_segments=clusters_all)
    starts = jnp.cumsum(counts) - counts
    window = 64
    padded = jnp.concatenate([sorted_index, jnp.zeros(window, jnp.int32)])
    label_ids = jnp.arange(LBL, dtype=jnp.int32)

    def per_cluster(back_rows, cluster_id):
        weight_now = lax.dynamic_index_in_dim(fine_weight, cluster_id, 0, keepdims=False)
        count_now = counts[cluster_id]
        start_now = starts[cluster_id]

        def per_window(block_index, carry):
            back_acc, weight_grad, loss_now = carry
            offset = block_index * window
            slot_ids = lax.dynamic_slice_in_dim(padded, (start_now + offset).astype(jnp.int32), window)
            usable = (offset + jnp.arange(window, dtype=jnp.int32)) < count_now
            row_ids = slot_ids // TOP
            in_row = slot_ids % TOP
            rows_now = encoded[row_ids]
            logits = jnp.dot(rows_now, weight_now.T, preferred_element_type=jnp.float32)
            truth = ((in_row == 0)[:, None] & (positive[row_ids][:, None] == label_ids[None, :])).astype(jnp.float32)
            mask = usable[:, None].astype(jnp.float32)
            loss_now = loss_now + jnp.sum(softplus_loss(logits, truth) * mask) / (TOP * LBL)
            grad_now = ((jax.nn.sigmoid(logits) - truth) / TOP * mask).astype(jnp.bfloat16)
            back_now = jnp.dot(grad_now, weight_now, preferred_element_type=jnp.float32).astype(jnp.bfloat16)
            back_acc = back_acc.at[row_ids].add(back_now.astype(jnp.float32))
            weight_grad = weight_grad + lax.dot_general(grad_now, rows_now, (((0,), (0,)), ((), ())), preferred_element_type=jnp.float32)
            return back_acc, weight_grad, loss_now

        blocks_now = (count_now + window - 1) // window
        start_carry = (back_rows, jnp.zeros((LBL, D), jnp.float32), jnp.zeros((), jnp.float32))
        back_rows, weight_grad, loss_now = lax.fori_loop(0, blocks_now, per_window, start_carry)
        return back_rows, (weight_grad.astype(jnp.bfloat16), loss_now)

    fine_back, outputs = lax.scan(per_cluster, jnp.zeros((row_total, D), jnp.float32), jnp.arange(clusters_all, dtype=jnp.int32))
    d_fine, cluster_loss = outputs
    d_encoded = (coarse_back + fine_back).astype(jnp.bfloat16)
    return row_loss, d_encoded, d_fine, cluster_loss
```

```python
import functools

import jax
import jax.numpy as jnp
from jax import lax
from jax.experimental import pallas as pl
from jax.experimental.pallas import tpu as pltpu
from jax.sharding import PartitionSpec as P


def per_device_exchange(encoded, coarse_weight, fine_weight, cluster_group, cluster_member, positive):
    row_dev, features = encoded.shape
    own_clusters = coarse_weight.shape[0]
    labels = fine_weight.shape[1]
    per_row = cluster_group.shape[1]
    dp_size = lax.axis_size("dp")
    label_size = lax.axis_size("label")
    device_total = dp_size * label_size
    cluster = cluster_group * own_clusters + cluster_member
    target = cluster[:, 0]
    full_weight = lax.all_gather(coarse_weight, ("dp", "label"), axis=0, tiled=True)
    scores = jnp.dot(encoded, full_weight.T, preferred_element_type=jnp.float32)
    column_ids = jnp.arange(scores.shape[1], dtype=jnp.int32)
    is_target = column_ids[None, :] == target[:, None]
    top_score = jnp.max(scores, axis=1, keepdims=True)
    logsum = top_score[:, 0] + jnp.log(jnp.sum(jnp.exp(scores - top_score), axis=1))
    target_score = jnp.sum(jnp.where(is_target, scores, 0.0), axis=1)
    coarse_grad = (jnp.exp(scores - logsum[:, None]) - is_target.astype(jnp.float32)).astype(
        jnp.bfloat16
    )
    coarse_back = jnp.dot(coarse_grad, full_weight, preferred_element_type=jnp.float32)
    row_loss = logsum - target_score
    capacity = max(2, 3 * row_dev * per_row // (2 * device_total))
    slot_count = row_dev * per_row
    group_ids = jnp.arange(device_total, dtype=jnp.int32)
    group_hit = (cluster_group[:, :, None] == group_ids[None, None, :]).astype(jnp.bfloat16)
    row_hit = jnp.sum(group_hit, axis=1)
    row_index = jnp.arange(row_dev, dtype=jnp.int32)
    strictly_lower = (row_index[:, None] > row_index[None, :]).astype(jnp.bfloat16)
    earlier_rows = jnp.dot(strictly_lower, row_hit, preferred_element_type=jnp.float32).astype(
        jnp.int32
    )
    ranking = jnp.take_along_axis(earlier_rows, cluster_group, axis=1)
    slot_place = (cluster_group * capacity + ranking).reshape(slot_count)
    slot_total = device_total * capacity
    in_row = jnp.arange(slot_count, dtype=jnp.int32) % per_row
    row_of = jnp.arange(slot_count, dtype=jnp.int32) // per_row
    slot_truth = jnp.where(in_row == 0, positive[row_of], -1)
    send_rows = (
        jnp.zeros((slot_total, features), jnp.bfloat16)
        .at[slot_place]
        .set(jnp.repeat(encoded, per_row, axis=0))
    )
    send_member = (
        jnp.full((slot_total,), float(own_clusters), jnp.float32)
        .at[slot_place]
        .set(cluster_member.reshape(slot_count).astype(jnp.float32))
    )
    send_truth = (
        jnp.full((slot_total,), -1.0, jnp.float32)
        .at[slot_place]
        .set(slot_truth.astype(jnp.float32))
    )
    recv_rows, recv_member, recv_truth = (
        lax.all_to_all(
            lax.all_to_all(
                send_rows.reshape(dp_size, label_size, capacity, features),
                "dp",
                split_axis=0,
                concat_axis=0,
                tiled=True,
            ),
            "label",
            split_axis=1,
            concat_axis=1,
            tiled=True,
        ),
        lax.all_to_all(
            lax.all_to_all(
                send_member.astype(jnp.bfloat16).reshape(dp_size, label_size, capacity),
                "dp",
                split_axis=0,
                concat_axis=0,
                tiled=True,
            ),
            "label",
            split_axis=1,
            concat_axis=1,
            tiled=True,
        ),
        lax.all_to_all(
            lax.all_to_all(
                send_truth.astype(jnp.bfloat16).reshape(dp_size, label_size, capacity),
                "dp",
                split_axis=0,
                concat_axis=0,
                tiled=True,
            ),
            "label",
            split_axis=1,
            concat_axis=1,
            tiled=True,
        ),
    )
    in_rows = recv_rows.reshape(slot_total, features)
    in_member = recv_member.reshape(slot_total).astype(jnp.int32)
    in_truth = recv_truth.reshape(slot_total).astype(jnp.int32)
    window = min(128, slot_total)
    turns = own_clusters + (slot_total + window - 1) // window
    sorted_index = jnp.argsort(in_member, stable=True)
    member_ids = jnp.arange(own_clusters, dtype=jnp.int32)
    counts = jnp.sum((in_member[:, None] == member_ids[None, :]).astype(jnp.int32), axis=0)
    starts = jnp.cumsum(counts) - counts
    blocks_each = (counts + window - 1) // window
    block_end = jnp.cumsum(blocks_each)
    block_start = block_end - blocks_each
    sorted_rows = jnp.concatenate(
        [in_rows[sorted_index], jnp.zeros((window, features), jnp.bfloat16)], axis=0
    )
    sorted_truth = jnp.concatenate([in_truth[sorted_index], jnp.full((window,), -1, jnp.int32)])
    label_ids = jnp.arange(labels, dtype=jnp.int32)
    window_ids = jnp.arange(window, dtype=jnp.int32)

    def visit(visit_index, carry):
        back_rows, weight_grads, losses = carry
        cluster_now = jnp.sum((block_end <= visit_index).astype(jnp.int32))
        active = cluster_now < own_clusters
        clamped = jnp.minimum(cluster_now, own_clusters - 1)
        offset = (visit_index - block_start[clamped]) * window
        base_row = starts[clamped] + offset
        usable = active & (offset + window_ids < counts[clamped])
        rows_now = lax.dynamic_slice_in_dim(sorted_rows, base_row, window, 0)
        truth_ids = lax.dynamic_slice_in_dim(sorted_truth, base_row, window, 0)
        weight_now = lax.dynamic_index_in_dim(fine_weight, clamped, 0, keepdims=False)
        logits = jnp.dot(rows_now, weight_now.T, preferred_element_type=jnp.float32)
        truth = (truth_ids[:, None] == label_ids[None, :]).astype(jnp.float32)
        mask = usable[:, None].astype(jnp.float32)
        bce = jnp.maximum(logits, 0.0) + jnp.log1p(jnp.exp(-jnp.abs(logits))) - truth * logits
        loss_now = jnp.sum(bce * mask) / (per_row * labels)
        grad_now = ((jax.nn.sigmoid(logits) - truth) / per_row * mask).astype(jnp.bfloat16)
        back_now = jnp.dot(grad_now, weight_now, preferred_element_type=jnp.float32).astype(
            jnp.bfloat16
        )
        current = lax.dynamic_slice_in_dim(back_rows, base_row, window, 0)
        back_rows = lax.dynamic_update_slice_in_dim(back_rows, current + back_now, base_row, 0)
        weight_step = lax.dot_general(
            grad_now, rows_now, (((0,), (0,)), ((), ())), preferred_element_type=jnp.float32
        )
        weight_grads = weight_grads.at[clamped].add(weight_step)
        losses = losses.at[clamped].add(loss_now)
        return (back_rows, weight_grads, losses)

    start_carry = (
        jnp.zeros((slot_total + window, features), jnp.bfloat16),
        jnp.zeros((own_clusters, labels, features), jnp.float32),
        jnp.zeros((own_clusters,), jnp.float32),
    )
    back_rows, weight_grads, cluster_loss = lax.fori_loop(0, turns, visit, start_carry)
    d_fine = weight_grads.astype(jnp.bfloat16)
    back_slots = (
        jnp.zeros((slot_total, features), jnp.bfloat16).at[sorted_index].set(back_rows[:slot_total])
    )
    returned = lax.all_to_all(
        lax.all_to_all(
            back_slots.reshape(dp_size, label_size, capacity, features),
            "dp",
            split_axis=0,
            concat_axis=0,
            tiled=True,
        ),
        "label",
        split_axis=1,
        concat_axis=1,
        tiled=True,
    )
    slot_back = returned.reshape(slot_total, features)[slot_place]
    fine_sum = jnp.sum(slot_back.reshape(row_dev, per_row, features).astype(jnp.float32), axis=1)
    d_encoded = (coarse_back + fine_sum).astype(jnp.bfloat16)
    return (row_loss, d_encoded, d_fine, cluster_loss)


SOURCES = 8


def fine_kernel(capacity, labels, me_ref, upper_ref, gathered_ref, weight_ref, part_ref, dfine_ref,
                loss_ref, sel, pick, member, truth, grad, back, total):
    step = pl.program_id(0)
    rows = part_ref.shape[1]
    features = part_ref.shape[2]
    slots = sel.shape[0]
    meta_at = gathered_ref.shape[1] - 16
    clusters = weight_ref.shape[0] // labels
    per_row = 8

    @pl.when(step == 0)
    def _():
        total[...] = jnp.zeros_like(total)
        loss_ref[...] = jnp.zeros_like(loss_ref)

    me = me_ref[0].astype(jnp.float32)
    hits, members, truths = [], [], []
    for i in range(SOURCES):
        meta = gathered_ref[i, meta_at:, :].astype(jnp.float32)
        hit = (meta[0:per_row, 0:rows] == me).astype(jnp.float32)
        hits.append(jnp.sum(hit, axis=0, keepdims=True))
        members.append(
            jnp.sum(hit * (meta[0:per_row, rows : 2 * rows] + 1.0), axis=0, keepdims=True)
        )
        truths.append(hit[0:1] * (meta[0:1, 2 * rows : 3 * rows] + 1.0))
    named = jnp.concatenate(hits, axis=0)
    rank = jnp.dot(named.astype(jnp.bfloat16), upper_ref[...], preferred_element_type=jnp.float32)
    rank = jnp.where(named > 0.0, rank, -1.0)
    place = lax.broadcasted_iota(jnp.int32, (capacity, rows), 0).astype(jnp.float32)
    for i in range(SOURCES):
        at = pl.ds(i * capacity, capacity)
        hot = (place == rank[i : i + 1, :]).astype(jnp.float32)
        pick[at, :] = hot.astype(jnp.bfloat16)
        sel[at, :] = jnp.dot(
            hot.astype(jnp.bfloat16), gathered_ref[i, 0:rows, :], preferred_element_type=jnp.float32
        ).astype(jnp.bfloat16)
        member[at, :] = jnp.broadcast_to(
            jnp.sum(hot * members[i], axis=1, keepdims=True) - 1.0, (capacity, labels)
        )
        truth[at, :] = jnp.broadcast_to(
            jnp.sum(hot * truths[i], axis=1, keepdims=True) - 1.0, (capacity, labels)
        )

    grad[...] = jnp.zeros_like(grad)

    @pl.loop(0, clusters // 2)
    def _(pair):
        first = (2 * pair).astype(jnp.float32)
        w = weight_ref[pl.ds(pl.multiple_of(pair * 2 * labels, 2 * labels), 2 * labels), :]
        both = lax.dot_general(
            sel[...], w, (((1,), (1,)), ((), ())), preferred_element_type=jnp.float32
        )
        mine = member[...]
        grad[...] = jnp.where(
            mine == first,
            both[:, :labels],
            jnp.where(mine == first + 1.0, both[:, labels:], grad[...]),
        )

    logits = grad[...]
    lane = lax.broadcasted_iota(jnp.int32, (slots, labels), 1).astype(jnp.float32)
    is_true = (lane == truth[...]).astype(jnp.float32)
    small = jnp.exp(-jnp.abs(logits))
    inverse = 1.0 / (1.0 + small)
    bce = jnp.maximum(logits, 0.0) + jnp.log1p(small) - is_true * logits
    row_bce = jnp.sum(bce, axis=1, keepdims=True)
    loss_ref[...] += jnp.sum(
        jnp.where(lane == member[...], row_bce, 0.0), axis=0, keepdims=True
    ) / (per_row * labels)
    grad[...] = (jnp.where(logits >= 0.0, inverse, small * inverse) - is_true) / per_row
    back[...] = jnp.zeros_like(back)

    @pl.loop(0, clusters // 2)
    def _(pair):
        first = (2 * pair).astype(jnp.float32)
        at = pl.ds(pl.multiple_of(pair * 2 * labels, 2 * labels), 2 * labels)
        mine = member[...]
        both = jnp.concatenate(
            [
                jnp.where(mine == first, grad[...], 0.0),
                jnp.where(mine == first + 1.0, grad[...], 0.0),
            ],
            axis=1,
        ).astype(jnp.bfloat16)
        back[...] += jnp.dot(both, weight_ref[at, :], preferred_element_type=jnp.float32)
        total[at, :] += lax.dot_general(
            both, sel[...], (((0,), (0,)), ((), ())), preferred_element_type=jnp.float32
        )

    for i in range(SOURCES):
        at = pl.ds(i * capacity, capacity)
        part_ref[i] = lax.dot_general(
            pick[at, :],
            back[at, :].astype(jnp.bfloat16),
            (((0,), (0,)), ((), ())),
            preferred_element_type=jnp.float32,
        ).astype(jnp.bfloat16)

    @pl.when(step == pl.num_programs(0) - 1)
    def _():
        dfine_ref[...] = total[...].astype(jnp.bfloat16)


def fine_part(gathered, fine_weight, me, rows, capacity):
    device_total, height, features = gathered.shape
    clusters, labels, _ = fine_weight.shape
    slots = SOURCES * capacity
    position = jnp.arange(rows, dtype=jnp.int32)
    upper = (position[:, None] < position[None, :]).astype(jnp.bfloat16)
    part, d_fine, loss = pl.pallas_call(
        functools.partial(fine_kernel, capacity, labels),
        grid=(device_total // SOURCES,),
        in_specs=[
            pl.BlockSpec(memory_space=pltpu.SMEM),
            pl.BlockSpec((rows, rows), lambda s: (0, 0)),
            pl.BlockSpec((SOURCES, height, features), lambda s: (s, 0, 0)),
            pl.BlockSpec((clusters * labels, features), lambda s: (0, 0)),
        ],
        out_specs=[
            pl.BlockSpec((SOURCES, rows, features), lambda s: (s, 0, 0)),
            pl.BlockSpec((clusters * labels, features), lambda s: (0, 0)),
            pl.BlockSpec((1, labels), lambda s: (0, 0)),
        ],
        out_shape=[
            jax.ShapeDtypeStruct((device_total, rows, features), jnp.bfloat16),
            jax.ShapeDtypeStruct((clusters * labels, features), jnp.bfloat16),
            jax.ShapeDtypeStruct((1, labels), jnp.float32),
        ],
        scratch_shapes=[
            pltpu.VMEM((slots, features), jnp.bfloat16),
            pltpu.VMEM((slots, rows), jnp.bfloat16),
            pltpu.VMEM((slots, labels), jnp.float32),
            pltpu.VMEM((slots, labels), jnp.float32),
            pltpu.VMEM((slots, labels), jnp.float32),
            pltpu.VMEM((slots, features), jnp.float32),
            pltpu.VMEM((clusters * labels, features), jnp.float32),
        ],
        compiler_params=pltpu.CompilerParams(vmem_limit_bytes=56 * 1024 * 1024),
        name="fine_part",
    )(me.reshape(1), upper, gathered, fine_weight.reshape(clusters * labels, features))
    return part, d_fine.reshape(clusters, labels, features), loss[0, :clusters]


def per_device_gather(encoded, coarse_weight, fine_weight, cluster_group, cluster_member, positive):
    rows, features = encoded.shape
    own_clusters = coarse_weight.shape[0]
    per_row = cluster_group.shape[1]
    device_total = lax.axis_size("dp") * lax.axis_size("label")
    me = lax.axis_index("dp") * lax.axis_size("label") + lax.axis_index("label")
    capacity = max(2, 3 * rows * per_row // (2 * device_total))
    meta = jnp.concatenate(
        [
            cluster_group.T,
            cluster_member.T,
            jnp.broadcast_to(positive[None, :], (per_row, rows)),
        ],
        axis=1,
    ).astype(jnp.bfloat16)
    meta = jnp.pad(meta, ((0, 16 - per_row), (0, features - 3 * rows)))
    block = jnp.concatenate([encoded, coarse_weight, meta], axis=0)
    gathered = collect(block)
    part, d_fine, cluster_loss = fine_part(gathered, fine_weight, me, rows, capacity)
    fine_sum = send_back(part)
    full_weight = gathered[:, rows : rows + own_clusters, :].reshape(-1, features)
    target = cluster_group[:, 0] * own_clusters + cluster_member[:, 0]
    scores = jnp.dot(encoded, full_weight.T, preferred_element_type=jnp.float32)
    column_ids = jnp.arange(scores.shape[1], dtype=jnp.int32)
    is_target = column_ids[None, :] == target[:, None]
    top_score = jnp.max(scores, axis=1, keepdims=True)
    logsum = top_score[:, 0] + jnp.log(jnp.sum(jnp.exp(scores - top_score), axis=1))
    target_score = jnp.sum(jnp.where(is_target, scores, 0.0), axis=1)
    coarse_grad = (jnp.exp(scores - logsum[:, None]) - is_target.astype(jnp.float32)).astype(
        jnp.bfloat16
    )
    coarse_back = jnp.dot(coarse_grad, full_weight, preferred_element_type=jnp.float32)
    d_encoded = (coarse_back + fine_sum.astype(jnp.float32)).astype(jnp.bfloat16)
    return logsum - target_score, d_encoded, d_fine, cluster_loss


def collect(block):
    return lax.all_gather(block, ("dp", "label"), axis=0, tiled=False)


def send_back(part):
    return lax.psum_scatter(part, ("dp", "label"), scatter_dimension=0, tiled=False)


def per_device(encoded, coarse_weight, fine_weight, cluster_group, cluster_member, positive):
    device_total = lax.axis_size("dp") * lax.axis_size("label")
    fits = device_total == 32 and encoded.shape[0] * 3 <= encoded.shape[1]
    plan = per_device_gather if fits else per_device_exchange
    return plan(encoded, coarse_weight, fine_weight, cluster_group, cluster_member, positive)


def solution(mesh):
    placed = (
        P(("dp", "label"), None),
        P(("dp", "label"), None),
        P(("dp", "label"), None, None),
        P(("dp", "label"), None),
        P(("dp", "label"), None),
        P(("dp", "label")),
    )
    return jax.shard_map(
        per_device,
        mesh=mesh,
        in_specs=placed,
        out_specs=(
            P(("dp", "label")),
            P(("dp", "label"), None),
            P(("dp", "label"), None, None),
            P(("dp", "label")),
        ),
        check_vma=False,
    )
```

```python
import functools

import jax
import jax.numpy as jnp
from jax import lax
from jax.experimental import pallas as pl
from jax.experimental.pallas import tpu as pltpu
from jax.sharding import PartitionSpec as P


def per_device_exchange(encoded, coarse_weight, fine_weight, cluster_group, cluster_member, positive):
    row_dev, features = encoded.shape
    own_clusters = coarse_weight.shape[0]
    labels = fine_weight.shape[1]
    per_row = cluster_group.shape[1]
    dp_size = lax.axis_size("dp")
    label_size = lax.axis_size("label")
    device_total = dp_size * label_size
    cluster = cluster_group * own_clusters + cluster_member
    target = cluster[:, 0]
    full_weight = lax.all_gather(coarse_weight, ("dp", "label"), axis=0, tiled=True)
    scores = jnp.dot(encoded, full_weight.T, preferred_element_type=jnp.float32)
    column_ids = jnp.arange(scores.shape[1], dtype=jnp.int32)
    is_target = column_ids[None, :] == target[:, None]
    top_score = jnp.max(scores, axis=1, keepdims=True)
    logsum = top_score[:, 0] + jnp.log(jnp.sum(jnp.exp(scores - top_score), axis=1))
    target_score = jnp.sum(jnp.where(is_target, scores, 0.0), axis=1)
    coarse_grad = (jnp.exp(scores - logsum[:, None]) - is_target.astype(jnp.float32)).astype(
        jnp.bfloat16
    )
    coarse_back = jnp.dot(coarse_grad, full_weight, preferred_element_type=jnp.float32)
    row_loss = logsum - target_score
    capacity = max(2, 3 * row_dev * per_row // (2 * device_total))
    slot_count = row_dev * per_row
    group_ids = jnp.arange(device_total, dtype=jnp.int32)
    group_hit = (cluster_group[:, :, None] == group_ids[None, None, :]).astype(jnp.bfloat16)
    row_hit = jnp.sum(group_hit, axis=1)
    row_index = jnp.arange(row_dev, dtype=jnp.int32)
    strictly_lower = (row_index[:, None] > row_index[None, :]).astype(jnp.bfloat16)
    earlier_rows = jnp.dot(strictly_lower, row_hit, preferred_element_type=jnp.float32).astype(
        jnp.int32
    )
    ranking = jnp.take_along_axis(earlier_rows, cluster_group, axis=1)
    slot_place = (cluster_group * capacity + ranking).reshape(slot_count)
    slot_total = device_total * capacity
    in_row = jnp.arange(slot_count, dtype=jnp.int32) % per_row
    row_of = jnp.arange(slot_count, dtype=jnp.int32) // per_row
    slot_truth = jnp.where(in_row == 0, positive[row_of], -1)
    send_rows = (
        jnp.zeros((slot_total, features), jnp.bfloat16)
        .at[slot_place]
        .set(jnp.repeat(encoded, per_row, axis=0))
    )
    send_member = (
        jnp.full((slot_total,), float(own_clusters), jnp.float32)
        .at[slot_place]
        .set(cluster_member.reshape(slot_count).astype(jnp.float32))
    )
    send_truth = (
        jnp.full((slot_total,), -1.0, jnp.float32)
        .at[slot_place]
        .set(slot_truth.astype(jnp.float32))
    )
    recv_rows, recv_member, recv_truth = (
        lax.all_to_all(
            lax.all_to_all(
                send_rows.reshape(dp_size, label_size, capacity, features),
                "dp",
                split_axis=0,
                concat_axis=0,
                tiled=True,
            ),
            "label",
            split_axis=1,
            concat_axis=1,
            tiled=True,
        ),
        lax.all_to_all(
            lax.all_to_all(
                send_member.astype(jnp.bfloat16).reshape(dp_size, label_size, capacity),
                "dp",
                split_axis=0,
                concat_axis=0,
                tiled=True,
            ),
            "label",
            split_axis=1,
            concat_axis=1,
            tiled=True,
        ),
        lax.all_to_all(
            lax.all_to_all(
                send_truth.astype(jnp.bfloat16).reshape(dp_size, label_size, capacity),
                "dp",
                split_axis=0,
                concat_axis=0,
                tiled=True,
            ),
            "label",
            split_axis=1,
            concat_axis=1,
            tiled=True,
        ),
    )
    in_rows = recv_rows.reshape(slot_total, features)
    in_member = recv_member.reshape(slot_total).astype(jnp.int32)
    in_truth = recv_truth.reshape(slot_total).astype(jnp.int32)
    window = min(128, slot_total)
    turns = own_clusters + (slot_total + window - 1) // window
    sorted_index = jnp.argsort(in_member, stable=True)
    member_ids = jnp.arange(own_clusters, dtype=jnp.int32)
    counts = jnp.sum((in_member[:, None] == member_ids[None, :]).astype(jnp.int32), axis=0)
    starts = jnp.cumsum(counts) - counts
    blocks_each = (counts + window - 1) // window
    block_end = jnp.cumsum(blocks_each)
    block_start = block_end - blocks_each
    sorted_rows = jnp.concatenate(
        [in_rows[sorted_index], jnp.zeros((window, features), jnp.bfloat16)], axis=0
    )
    sorted_truth = jnp.concatenate([in_truth[sorted_index], jnp.full((window,), -1, jnp.int32)])
    label_ids = jnp.arange(labels, dtype=jnp.int32)
    window_ids = jnp.arange(window, dtype=jnp.int32)

    def visit(visit_index, carry):
        back_rows, weight_grads, losses = carry
        cluster_now = jnp.sum((block_end <= visit_index).astype(jnp.int32))
        active = cluster_now < own_clusters
        clamped = jnp.minimum(cluster_now, own_clusters - 1)
        offset = (visit_index - block_start[clamped]) * window
        base_row = starts[clamped] + offset
        usable = active & (offset + window_ids < counts[clamped])
        rows_now = lax.dynamic_slice_in_dim(sorted_rows, base_row, window, 0)
        truth_ids = lax.dynamic_slice_in_dim(sorted_truth, base_row, window, 0)
        weight_now = lax.dynamic_index_in_dim(fine_weight, clamped, 0, keepdims=False)
        logits = jnp.dot(rows_now, weight_now.T, preferred_element_type=jnp.float32)
        truth = (truth_ids[:, None] == label_ids[None, :]).astype(jnp.float32)
        mask = usable[:, None].astype(jnp.float32)
        bce = jnp.maximum(logits, 0.0) + jnp.log1p(jnp.exp(-jnp.abs(logits))) - truth * logits
        loss_now = jnp.sum(bce * mask) / (per_row * labels)
        grad_now = ((jax.nn.sigmoid(logits) - truth) / per_row * mask).astype(jnp.bfloat16)
        back_now = jnp.dot(grad_now, weight_now, preferred_element_type=jnp.float32).astype(
            jnp.bfloat16
        )
        current = lax.dynamic_slice_in_dim(back_rows, base_row, window, 0)
        back_rows = lax.dynamic_update_slice_in_dim(back_rows, current + back_now, base_row, 0)
        weight_step = lax.dot_general(
            grad_now, rows_now, (((0,), (0,)), ((), ())), preferred_element_type=jnp.float32
        )
        weight_grads = weight_grads.at[clamped].add(weight_step)
        losses = losses.at[clamped].add(loss_now)
        return (back_rows, weight_grads, losses)

    start_carry = (
        jnp.zeros((slot_total + window, features), jnp.bfloat16),
        jnp.zeros((own_clusters, labels, features), jnp.float32),
        jnp.zeros((own_clusters,), jnp.float32),
    )
    back_rows, weight_grads, cluster_loss = lax.fori_loop(0, turns, visit, start_carry)
    d_fine = weight_grads.astype(jnp.bfloat16)
    back_slots = (
        jnp.zeros((slot_total, features), jnp.bfloat16).at[sorted_index].set(back_rows[:slot_total])
    )
    returned = lax.all_to_all(
        lax.all_to_all(
            back_slots.reshape(dp_size, label_size, capacity, features),
            "dp",
            split_axis=0,
            concat_axis=0,
            tiled=True,
        ),
        "label",
        split_axis=1,
        concat_axis=1,
        tiled=True,
    )
    slot_back = returned.reshape(slot_total, features)[slot_place]
    fine_sum = jnp.sum(slot_back.reshape(row_dev, per_row, features).astype(jnp.float32), axis=1)
    d_encoded = (coarse_back + fine_sum).astype(jnp.bfloat16)
    return (row_loss, d_encoded, d_fine, cluster_loss)


SOURCES = 8
TOGETHER = 8


def fine_kernel(capacity, labels, me_ref, upper_ref, gathered_ref, weight_ref, part_ref, dfine_ref,
                loss_ref, sel, pick, member, truth, grad, back, total):
    step = pl.program_id(0)
    rows = part_ref.shape[1]
    features = part_ref.shape[2]
    slots = sel.shape[0]
    meta_at = gathered_ref.shape[1] - 16
    clusters = weight_ref.shape[0] // labels
    per_row = 8

    @pl.when(step == 0)
    def _():
        total[...] = jnp.zeros_like(total)
        loss_ref[...] = jnp.zeros_like(loss_ref)

    me = me_ref[0].astype(jnp.float32)
    hits, members, truths = [], [], []
    for i in range(SOURCES):
        meta = gathered_ref[i, meta_at:, :].astype(jnp.float32)
        hit = (meta[0:per_row, 0:rows] == me).astype(jnp.float32)
        hits.append(jnp.sum(hit, axis=0, keepdims=True))
        members.append(
            jnp.sum(hit * (meta[0:per_row, rows : 2 * rows] + 1.0), axis=0, keepdims=True)
        )
        truths.append(hit[0:1] * (meta[0:1, 2 * rows : 3 * rows] + 1.0))
    named = jnp.concatenate(hits, axis=0)
    rank = jnp.dot(named.astype(jnp.bfloat16), upper_ref[...], preferred_element_type=jnp.float32)
    rank = jnp.where(named > 0.0, rank, -1.0)
    place = lax.broadcasted_iota(jnp.int32, (capacity, rows), 0).astype(jnp.float32)
    for i in range(SOURCES):
        at = pl.ds(i * capacity, capacity)
        hot = (place == rank[i : i + 1, :]).astype(jnp.float32)
        pick[at, :] = hot.astype(jnp.bfloat16)
        sel[at, :] = jnp.dot(
            hot.astype(jnp.bfloat16), gathered_ref[i, 0:rows, :], preferred_element_type=jnp.float32
        ).astype(jnp.bfloat16)
        member[at, :] = jnp.broadcast_to(
            jnp.sum(hot * members[i], axis=1, keepdims=True) - 1.0, (capacity, labels)
        )
        truth[at, :] = jnp.broadcast_to(
            jnp.sum(hot * truths[i], axis=1, keepdims=True) - 1.0, (capacity, labels)
        )

    grad[...] = jnp.zeros_like(grad)

    span = TOGETHER * labels

    @pl.loop(0, clusters // TOGETHER)
    def _(group):
        first = (TOGETHER * group).astype(jnp.float32)
        w = weight_ref[pl.ds(pl.multiple_of(group * span, span), span), :]
        every = lax.dot_general(
            sel[...], w, (((1,), (1,)), ((), ())), preferred_element_type=jnp.float32
        )
        mine = member[...]
        kept = grad[...]
        for j in range(TOGETHER):
            kept = jnp.where(mine == first + j, every[:, j * labels : (j + 1) * labels], kept)
        grad[...] = kept

    logits = grad[...]
    lane = lax.broadcasted_iota(jnp.int32, (slots, labels), 1).astype(jnp.float32)
    is_true = (lane == truth[...]).astype(jnp.float32)
    small = jnp.exp(-jnp.abs(logits))
    inverse = 1.0 / (1.0 + small)
    bce = jnp.maximum(logits, 0.0) + jnp.log1p(small) - is_true * logits
    row_bce = jnp.sum(bce, axis=1, keepdims=True)
    loss_ref[...] += jnp.sum(
        jnp.where(lane == member[...], row_bce, 0.0), axis=0, keepdims=True
    ) / (per_row * labels)
    grad[...] = (jnp.where(logits >= 0.0, inverse, small * inverse) - is_true) / per_row
    back[...] = jnp.zeros_like(back)

    @pl.loop(0, clusters // TOGETHER)
    def _(group):
        first = (TOGETHER * group).astype(jnp.float32)
        at = pl.ds(pl.multiple_of(group * span, span), span)
        mine = member[...]
        own = grad[...]
        every = jnp.concatenate(
            [jnp.where(mine == first + j, own, 0.0) for j in range(TOGETHER)], axis=1
        ).astype(jnp.bfloat16)
        back[...] += jnp.dot(every, weight_ref[at, :], preferred_element_type=jnp.float32)
        total[at, :] += lax.dot_general(
            every, sel[...], (((0,), (0,)), ((), ())), preferred_element_type=jnp.float32
        )

    for i in range(SOURCES):
        at = pl.ds(i * capacity, capacity)
        part_ref[i] = lax.dot_general(
            pick[at, :],
            back[at, :].astype(jnp.bfloat16),
            (((0,), (0,)), ((), ())),
            preferred_element_type=jnp.float32,
        ).astype(jnp.bfloat16)

    @pl.when(step == pl.num_programs(0) - 1)
    def _():
        dfine_ref[...] = total[...].astype(jnp.bfloat16)


def fine_part(gathered, fine_weight, me, rows, capacity):
    device_total, height, features = gathered.shape
    clusters, labels, _ = fine_weight.shape
    slots = SOURCES * capacity
    position = jnp.arange(rows, dtype=jnp.int32)
    upper = (position[:, None] < position[None, :]).astype(jnp.bfloat16)
    part, d_fine, loss = pl.pallas_call(
        functools.partial(fine_kernel, capacity, labels),
        grid=(device_total // SOURCES,),
        in_specs=[
            pl.BlockSpec(memory_space=pltpu.SMEM),
            pl.BlockSpec((rows, rows), lambda s: (0, 0)),
            pl.BlockSpec((SOURCES, height, features), lambda s: (s, 0, 0)),
            pl.BlockSpec((clusters * labels, features), lambda s: (0, 0)),
        ],
        out_specs=[
            pl.BlockSpec((SOURCES, rows, features), lambda s: (s, 0, 0)),
            pl.BlockSpec((clusters * labels, features), lambda s: (0, 0)),
            pl.BlockSpec((1, labels), lambda s: (0, 0)),
        ],
        out_shape=[
            jax.ShapeDtypeStruct((device_total, rows, features), jnp.bfloat16),
            jax.ShapeDtypeStruct((clusters * labels, features), jnp.bfloat16),
            jax.ShapeDtypeStruct((1, labels), jnp.float32),
        ],
        scratch_shapes=[
            pltpu.VMEM((slots, features), jnp.bfloat16),
            pltpu.VMEM((slots, rows), jnp.bfloat16),
            pltpu.VMEM((slots, labels), jnp.float32),
            pltpu.VMEM((slots, labels), jnp.float32),
            pltpu.VMEM((slots, labels), jnp.float32),
            pltpu.VMEM((slots, features), jnp.float32),
            pltpu.VMEM((clusters * labels, features), jnp.float32),
        ],
        compiler_params=pltpu.CompilerParams(vmem_limit_bytes=56 * 1024 * 1024),
        name="fine_part",
    )(me.reshape(1), upper, gathered, fine_weight.reshape(clusters * labels, features))
    return part, d_fine.reshape(clusters, labels, features), loss[0, :clusters]


def per_device_gather(encoded, coarse_weight, fine_weight, cluster_group, cluster_member, positive):
    rows, features = encoded.shape
    own_clusters = coarse_weight.shape[0]
    per_row = cluster_group.shape[1]
    device_total = lax.axis_size("dp") * lax.axis_size("label")
    me = lax.axis_index("dp") * lax.axis_size("label") + lax.axis_index("label")
    capacity = max(2, 3 * rows * per_row // (2 * device_total))
    meta = jnp.concatenate(
        [
            cluster_group.T,
            cluster_member.T,
            jnp.broadcast_to(positive[None, :], (per_row, rows)),
        ],
        axis=1,
    ).astype(jnp.bfloat16)
    meta = jnp.pad(meta, ((0, 16 - per_row), (0, features - 3 * rows)))
    block = jnp.concatenate([encoded, coarse_weight, meta], axis=0)
    gathered = collect(block)
    part, d_fine, cluster_loss = fine_part(gathered, fine_weight, me, rows, capacity)
    fine_sum = send_back(part)
    full_weight = gathered[:, rows : rows + own_clusters, :].reshape(-1, features)
    target = cluster_group[:, 0] * own_clusters + cluster_member[:, 0]
    scores = jnp.dot(encoded, full_weight.T, preferred_element_type=jnp.float32)
    column_ids = jnp.arange(scores.shape[1], dtype=jnp.int32)
    is_target = column_ids[None, :] == target[:, None]
    top_score = jnp.max(scores, axis=1, keepdims=True)
    logsum = top_score[:, 0] + jnp.log(jnp.sum(jnp.exp(scores - top_score), axis=1))
    target_score = jnp.sum(jnp.where(is_target, scores, 0.0), axis=1)
    coarse_grad = (jnp.exp(scores - logsum[:, None]) - is_target.astype(jnp.float32)).astype(
        jnp.bfloat16
    )
    coarse_back = jnp.dot(coarse_grad, full_weight, preferred_element_type=jnp.float32)
    d_encoded = (coarse_back + fine_sum.astype(jnp.float32)).astype(jnp.bfloat16)
    return logsum - target_score, d_encoded, d_fine, cluster_loss


MESH = pl.DeviceIdType.MESH


class Around:
    def __init__(self):
        self.dp = lax.axis_index("dp")
        self.label = lax.axis_index("label")
        self.z = self.label // 2
        self.core = self.label % 2
        self.depth = lax.axis_size("label") // 2
        self.line = (self.dp // 2) * 2 + 1 - self.dp % 2
        self.column = (1 - self.dp // 2) * 2 + self.dp % 2
        self.corner = 3 - self.dp
        self.x = (self.line, self.label)
        self.y = (self.column, self.label)
        self.sibling = (self.dp, self.z * 2 + 1 - self.core)
        self.left = (self.dp, self.label - 2)
        self.right = (self.dp, self.label + 2)
        self.has_left = self.z > 0
        self.has_right = self.z < self.depth - 1
        self.pending = []

    def greet(self):
        barrier = pltpu.get_barrier_semaphore()
        for other in (self.x, self.y, self.sibling):
            pl.semaphore_signal(barrier, inc=1, device_id=other, device_id_type=MESH)

        @pl.when(self.has_left)
        def _():
            pl.semaphore_signal(barrier, inc=1, device_id=self.left, device_id_type=MESH)

        @pl.when(self.has_right)
        def _():
            pl.semaphore_signal(barrier, inc=1, device_id=self.right, device_id_type=MESH)

        lefts = lax.div(self.z + self.depth - 1, self.depth)
        rights = lax.div(2 * (self.depth - 1) - self.z, self.depth)
        pl.semaphore_wait(barrier, 3 + lefts + rights)

    def at_distance(self, k):
        if k == 0:
            return [(None, self.z, 0)]
        return [
            (self.z >= k, self.z - k, -1),
            (self.z + k < self.depth, self.z + k, 1),
        ]

    def send(self, when, make):
        guarded(when, lambda: make().start())
        self.pending.append((when, make))

    def finish(self):
        for when, make in self.pending:
            guarded(when, lambda make=make: make().wait_send())


def guarded(when, action):
    if when is None:
        action()
    else:
        pl.when(when)(action)


def both_true(first, second):
    return second if first is None else jnp.logical_and(first, second)


def remote(src, dst, send_sem, recv_sem, device):
    return pltpu.make_async_remote_copy(
        src_ref=src,
        dst_ref=dst,
        send_sem=send_sem,
        recv_sem=recv_sem,
        device_id=device,
        device_id_type=MESH,
    )


def gather_kernel(block_ref, out_ref, own_sem, sz, sx, sy, sa, sb, ss, rz, rx, ry, ra, rb, rs):
    here = Around()
    half = block_ref.shape[0] // 2
    depth = here.depth

    def place(dp, z, core):
        return out_ref.at[(dp * depth + z) * 2 + core]

    own = pltpu.make_async_copy(block_ref, place(here.dp, here.z, here.core), own_sem)
    own.start()
    here.greet()
    halves = (pl.ds(0, half), pl.ds(half, half))

    def full(dp, z, send_sem, recv_sem, device, mine=False):
        spot = place(dp, z, here.core)
        src = block_ref if mine else spot
        return lambda: remote(src, spot, send_sem, recv_sem, device)

    def part(dp, z, which, send_sem, recv_sem, device):
        spot = place(dp, z, here.core).at[halves[which]]
        return lambda: remote(spot, spot, send_sem, recv_sem, device)

    def to_sibling(when, dp, z, mine=False):
        n = dp * depth + z
        here.send(when, full(dp, z, ss.at[n], rs.at[n], here.sibling, mine))

    def along_z(k):
        for when, z, side in here.at_distance(k):
            mine = side == 0
            if not mine:
                guarded(when, lambda z=z: full(here.dp, z, sz.at[0, z], rz.at[z], here.left)().wait_recv())
            if side <= 0:
                here.send(
                    both_true(when, here.has_right),
                    full(here.dp, z, sz.at[1, z], rz.at[z], here.right, mine),
                )
            if side >= 0:
                here.send(
                    both_true(when, here.has_left),
                    full(here.dp, z, sz.at[0, z], rz.at[z], here.left, mine),
                )
            here.send(when, full(here.dp, z, sx.at[z], rx.at[z], here.x, mine))
            here.send(when, full(here.dp, z, sy.at[z], ry.at[z], here.y, mine))
            to_sibling(when, here.dp, z, mine)

    def turn(k):
        for when, z, _ in here.at_distance(k):
            guarded(when, lambda z=z: full(here.line, z, sx.at[z], rx.at[z], here.x)().wait_recv())
            here.send(when, part(here.line, z, 0, sa.at[z], ra.at[z], here.y))
            to_sibling(when, here.line, z)
            guarded(when, lambda z=z: full(here.column, z, sy.at[z], ry.at[z], here.y)().wait_recv())
            here.send(when, part(here.column, z, 1, sb.at[z], rb.at[z], here.x))
            to_sibling(when, here.column, z)

    def corner(k):
        for when, z, _ in here.at_distance(k):
            guarded(when, lambda z=z: part(here.corner, z, 0, sa.at[z], ra.at[z], here.y)().wait_recv())
            guarded(when, lambda z=z: part(here.corner, z, 1, sb.at[z], rb.at[z], here.x)().wait_recv())
            to_sibling(when, here.corner, z)

    along_z(0)
    for k in range(1, depth):
        along_z(k)
        turn(k - 1)
        if k > 1:
            corner(k - 2)
    turn(depth - 1)
    corner(depth - 2)
    corner(depth - 1)

    for n in range(4 * depth):
        spot = out_ref.at[n * 2 + 1 - here.core]
        remote(spot, spot, ss.at[n], rs.at[n], here.sibling).wait_recv()
    here.finish()
    own.wait()


def collect(block):
    depth = lax.axis_size("label") // 2
    sems = pltpu.SemaphoreType.DMA
    line = sems((depth,))
    return pl.pallas_call(
        gather_kernel,
        in_specs=[pl.BlockSpec(memory_space=pl.ANY)],
        out_specs=pl.BlockSpec(memory_space=pl.ANY),
        out_shape=jax.ShapeDtypeStruct((8 * depth,) + block.shape, block.dtype),
        scratch_shapes=[sems, sems((2, depth)), line, line, line, line, sems((4 * depth,))]
        + [line, line, line, line, line, sems((4 * depth,))],
        compiler_params=pltpu.CompilerParams(collective_id=0, has_side_effects=True),
        name="gather_rows",
    )(block)


def scatter_kernel(part_ref, out_ref, arrived, acc, ina, inb, inx, iny, inz, total,
                   sz, sx, sy, sa, sb, ss, rz, rx, ry, ra, rb, rs):
    here = Around()
    depth = here.depth
    rows = out_ref.shape[0]
    half = rows // 2
    tile = 64 if half % 64 == 0 else 16
    halves = (pl.ds(0, half), pl.ds(half, half))
    here.greet()

    def sibling_copy(n, core):
        return remote(
            part_ref.at[n * 2 + core], arrived.at[n], ss.at[n], rs.at[n], here.sibling
        )

    order = [here.corner, here.line, here.column, here.dp]
    for k in range(depth - 1, -1, -1):
        for when, z, _ in here.at_distance(k):
            for dp in order:
                here.send(
                    when,
                    lambda n=dp * depth + z: sibling_copy(n, 1 - here.core),
                )

    def add(dst, first, others, start=0, count=rows):
        @pl.loop(0, count // tile)
        def _(i):
            at = pl.ds(pl.multiple_of(i * tile, tile) + start, tile)
            inner = pl.ds(pl.multiple_of(i * tile, tile), tile)
            value = first[at, :].astype(jnp.float32)
            for other in others:
                value = value + other[inner, :].astype(jnp.float32)
            dst[at, :] = value.astype(dst.dtype)

    def send_a(z):
        n = here.corner * depth + z
        return remote(acc.at[n, halves[0]], ina.at[z], sa.at[z], ra.at[z], here.y)

    def send_b(z):
        n = here.corner * depth + z
        return remote(acc.at[n, halves[1]], inb.at[z], sb.at[z], rb.at[z], here.x)

    def send_x(z):
        return remote(acc.at[here.line * depth + z], inx.at[z], sx.at[z], rx.at[z], here.x)

    def send_y(z):
        return remote(acc.at[here.column * depth + z], iny.at[z], sy.at[z], ry.at[z], here.y)

    def send_right(z):
        return remote(total.at[z], inz.at[0, z], sz.at[0, z], rz.at[0, z], here.right)

    def send_left(z):
        return remote(total.at[z], inz.at[1, z], sz.at[1, z], rz.at[1, z], here.left)

    def cores(k):
        for when, z, _ in here.at_distance(k):
            for dp in order:

                def one(n=dp * depth + z):
                    sibling_copy(n, 1 - here.core).wait_recv()
                    add(acc.at[n], part_ref.at[n * 2 + here.core], [arrived.at[n]])

                guarded(when, one)
                if dp is here.corner:
                    here.send(when, lambda z=z: send_a(z))
                    here.send(when, lambda z=z: send_b(z))

    def turn(k):
        for when, z, _ in here.at_distance(k):

            def first(z=z):
                send_a(z).wait_recv()
                spot = acc.at[here.line * depth + z]
                add(spot, spot, [ina.at[z]], 0, half)

            guarded(when, first)
            here.send(when, lambda z=z: send_x(z))

            def second(z=z):
                send_b(z).wait_recv()
                spot = acc.at[here.column * depth + z]
                add(spot, spot, [inb.at[z]], half, half)

            guarded(when, second)
            here.send(when, lambda z=z: send_y(z))

    def along_z(k):
        for when, z, side in here.at_distance(k):

            def quad(z=z):
                send_x(z).wait_recv()
                send_y(z).wait_recv()
                dst = out_ref if side == 0 else total.at[z]
                add(dst, acc.at[here.dp * depth + z], [inx.at[z], iny.at[z]])

            guarded(when, quad)
            dst = out_ref if side == 0 else total.at[z]
            if side >= 0:

                def from_left(z=z, dst=dst):
                    send_right(z).wait_recv()
                    add(dst, dst, [inz.at[0, z]])

                guarded(both_true(when, here.has_left), from_left)
            if side <= 0:

                def from_right(z=z, dst=dst):
                    send_left(z).wait_recv()
                    add(dst, dst, [inz.at[1, z]])

                guarded(both_true(when, here.has_right), from_right)
            if side > 0:
                here.send(when, lambda z=z: send_right(z))
            if side < 0:
                here.send(when, lambda z=z: send_left(z))

    far = depth - 1
    for step in range(depth + 2):
        if step < depth:
            cores(far - step)
        if 0 <= step - 1 < depth:
            turn(far - step + 1)
        if 0 <= step - 2 < depth:
            along_z(far - step + 2)
    here.finish()


def send_back(part):
    depth = lax.axis_size("label") // 2
    _, rows, features = part.shape
    sems = pltpu.SemaphoreType.DMA
    line = sems((depth,))
    kind = part.dtype
    return pl.pallas_call(
        scatter_kernel,
        in_specs=[pl.BlockSpec(memory_space=pltpu.VMEM)],
        out_specs=pl.BlockSpec(memory_space=pltpu.VMEM),
        out_shape=jax.ShapeDtypeStruct((rows, features), jnp.float32),
        scratch_shapes=[
            pltpu.VMEM((4 * depth, rows, features), kind),
            pltpu.VMEM((4 * depth, rows, features), kind),
            pltpu.VMEM((depth, rows // 2, features), kind),
            pltpu.VMEM((depth, rows // 2, features), kind),
            pltpu.VMEM((depth, rows, features), kind),
            pltpu.VMEM((depth, rows, features), kind),
            pltpu.VMEM((2, depth, rows, features), kind),
            pltpu.VMEM((depth, rows, features), kind),
        ]
        + [sems((2, depth)), line, line, line, line, sems((4 * depth,))]
        + [sems((2, depth)), line, line, line, line, sems((4 * depth,))],
        compiler_params=pltpu.CompilerParams(
            collective_id=1, has_side_effects=True, vmem_limit_bytes=56 * 1024 * 1024
        ),
        name="return_rows",
    )(part)


def per_device(encoded, coarse_weight, fine_weight, cluster_group, cluster_member, positive):
    device_total = lax.axis_size("dp") * lax.axis_size("label")
    fits = device_total == 32 and encoded.shape[0] * 3 <= encoded.shape[1]
    plan = per_device_gather if fits else per_device_exchange
    return plan(encoded, coarse_weight, fine_weight, cluster_group, cluster_member, positive)


def solution(mesh):
    placed = (
        P(("dp", "label"), None),
        P(("dp", "label"), None),
        P(("dp", "label"), None, None),
        P(("dp", "label"), None),
        P(("dp", "label"), None),
        P(("dp", "label")),
    )
    return jax.shard_map(
        per_device,
        mesh=mesh,
        in_specs=placed,
        out_specs=(
            P(("dp", "label")),
            P(("dp", "label"), None),
            P(("dp", "label"), None, None),
            P(("dp", "label")),
        ),
        check_vma=False,
    )
```
